32 devices in a mesh: ctx: 8 (over z, y), tp: 4 (over x, core).
Axes of the slice: x: 2, y: 2, z: 4, core: 2. Of those that a mesh axis runs over, the one named last changes fastest.
Arguments:
- query: bfloat16 [1024, 8192], P('ctx', 'tp'), may hold values from -6 to 6
- key: bfloat16 [1024, 512], P('ctx', 'tp'), may hold values from -6 to 6
- value: bfloat16 [1024, 512], P('ctx', 'tp'), may hold values from -6 to 6
- out_grad: bfloat16 [1024, 8192], P('ctx', 'tp'), may hold values from -6 to 6
- hidden_in: bfloat16 [1024, 8192], P('ctx', 'tp'), may hold values from -0.119628906 to 0.119628906
- segment_ids: int32 [1024], P('ctx'), may hold values from 0 to 3, as said below
Outputs:
- query_grad: bfloat16 [1024, 8192], P('ctx', 'tp')
- key_grad: bfloat16 [1024, 512], P('ctx', 'tp')
- value_grad: bfloat16 [1024, 512], P('ctx', 'tp')
- value_weight_grad: float32 [8192, 512], P('ctx', 'tp')
The draws below stay inside these ranges and needn't reach their ends.
Inputs may be any that keep to these rules, and one draw needn't show every extreme that they name: `segment_ids`: ids never fall; document 0 holds 32 to 96 tokens, document 1 exactly 512 tokens, every later document at least one token and fewer than 512.
All inputs are finite; a program needn't handle non-finite values.
Results may differ from the reference program's by a relative error of at most 0.028.
Values may be sent and summed in bfloat16 or wider, within the bound.
A program may use at most 64 MiB of HBM per device.

```python
import math
import jax
import jax.numpy as jnp
from jax import lax

D = 8192
QH = 64
KH = 4
HD = 128
TOK_DEV = 128
TOKENS = 1024
N_CTX = 8


def beacon_row(key):
    picks = jax.random.bernoulli(jax.random.fold_in(key, 7), 0.5, (HD,))
    return jnp.where(picks, 1.0, -1.0).astype(jnp.float32)


def document_layout(key):
    key = jax.random.fold_in(key, 5)
    first_key, cut_key = jax.random.split(key)
    first_length = jax.random.randint(first_key, (), TOK_DEV // 4, 3 * TOK_DEV // 4 + 1, dtype=jnp.int32)
    shuffled = jax.random.permutation(cut_key, TOKENS // 2 - TOK_DEV).astype(jnp.int32)
    cuts = shuffled[:N_CTX // 2 - 3] + 1
    return (first_length, cuts)


def draw_segment_ids(key, part):
    first_length, cuts = document_layout(key)
    positions = jnp.arange(TOKENS, dtype=jnp.int32)
    after = positions - first_length - TOKENS // 2
    later = 2 + jnp.sum((cuts[None, :] <= after[:, None]).astype(jnp.int32), axis=1)
    inner = jnp.where(after < 0, 1, later)
    return jnp.where(positions < first_length, 0, inner).astype(jnp.int32)


def draw_key(key, part):
    beacon = beacon_row(key)
    first_length, cuts = document_layout(key)
    key = jax.random.fold_in(key, 11)
    positions = jnp.arange(TOKENS, dtype=jnp.int32)
    anchored = (positions >= first_length) & (positions < TOK_DEV)
    drawn = jax.random.truncated_normal(key, -4.0, 4.0, (TOKENS, KH, HD), jnp.float32)
    result = drawn + jnp.where(anchored[:, None, None], beacon[None, None, :], 0.0)
    return result.reshape(TOKENS, KH * HD).astype(jnp.bfloat16)


def draw_query(key, part):
    beacon = beacon_row(key)
    key = jax.random.fold_in(key, 23)
    lean = (math.log(N_CTX) + 0.5) / math.sqrt(HD)
    drawn = jax.random.truncated_normal(key, -4.0, 4.0, (TOKENS, QH, HD), jnp.float32)
    result = drawn + lean * beacon[None, None, :]
    return result.reshape(TOKENS, QH * HD).astype(jnp.bfloat16)


def raised(drawn, own_key, source, target, parts, factor):
    owner, partner = [(jnp.arange(drawn.shape[axis_at]) // (drawn.shape[axis_at] // parts)).reshape([-1 if axis == axis_at else 1 for axis in range(drawn.ndim)]) for axis_at in (source, target)]
    chosen = jax.random.permutation(own_key, parts)[partner]
    strong = (owner == chosen) | (owner == (partner + parts // 2) % parts)
    return jnp.where(strong, factor * drawn, drawn)


def block_scale(stream_key, extent, cuts, low, top_value):
    factor_of = 1.0
    for dim, parts in cuts:
        draws = jax.random.uniform(jax.random.fold_in(jax.random.fold_in(stream_key, 6), dim), (parts,), jnp.float32, low / len(cuts), top_value / len(cuts))
        factor_of = factor_of * jnp.repeat(jnp.exp(draws), extent[dim] // parts).reshape((-1,) + (1,) * (len(extent) - 1 - dim))
    return factor_of


def centred(rng, shape, spread, reach, cuts=(), held_as=jnp.bfloat16):
    entries = jax.random.normal(rng, shape, jnp.float32) * spread
    if len(cuts) > 0:
        entries = block_scale(rng, shape, cuts, -0.22, 0.18) * entries
    return jnp.clip(entries, min=-reach, max=reach).astype(held_as)


def noise_with(rng, extent, deviation, most, cuts, heavy, kind=jnp.bfloat16):
    values = deviation * jax.random.normal(rng, extent, jnp.float32)
    if cuts:
        values = values * block_scale(rng, extent, cuts, -0.22, 0.18)
    return jnp.clip(raised(values, jax.random.fold_in(rng, 3), *heavy), -most, most).astype(kind)


def setup_inputs(seed: int = 0) -> dict:
    arg_keys = jax.random.split(jax.random.key(seed), 7)
    return {
        "query": draw_query(jax.random.fold_in(arg_keys[6], 71), 0),
        "key": draw_key(jax.random.fold_in(arg_keys[6], 71), 0),
        "value": centred(arg_keys[2], (TOKENS, KH * HD), 1.0, 6.0, ((0, 8), (1, 4))),
        "out_grad": centred(arg_keys[3], (TOKENS, QH * HD), 1.0, 6.0, ((0, 8), (1, 4))),
        "hidden_in": noise_with(arg_keys[4], (TOKENS, D), 0.02, 0.119628906, ((0, 8), (1, 4)), (0, 1, 8, 2.0)),
        "segment_ids": draw_segment_ids(jax.random.fold_in(arg_keys[6], 71), 0),
    }


def attend_group(query_group, key_group, value_group, grad_group, segments):
    positions = jnp.arange(TOKENS, dtype=jnp.int32)
    score_scale = HD ** -0.5
    block_rows = min(512, TOKENS)
    block_count = TOKENS // block_rows
    key_wide = key_group.astype(jnp.float32)
    value_wide = value_group.astype(jnp.float32)

    def one_block(carry, block_idx):
        key_acc, value_acc = carry
        start = (block_idx * block_rows).astype(jnp.int32)
        query_block = lax.dynamic_slice_in_dim(query_group, start, block_rows, 0).astype(jnp.float32)
        grad_block = lax.dynamic_slice_in_dim(grad_group, start, block_rows, 0).astype(jnp.float32)
        query_pos = start + jnp.arange(block_rows, dtype=jnp.int32)
        query_seg = lax.dynamic_slice_in_dim(segments, start, block_rows, 0)
        allowed = (positions[None, :] <= query_pos[:, None]) & (segments[None, :] == query_seg[:, None])
        scores = jnp.einsum('tgd,ud->gtu', query_block, key_wide) * score_scale
        scores = jnp.where(allowed[None], scores, -jnp.inf)
        peak = jnp.max(scores, axis=-1, keepdims=True)
        log_total = peak + jnp.log(jnp.sum(jnp.exp(scores - peak), axis=-1, keepdims=True))
        probs = jnp.exp(scores - log_total)
        probs_low = lax.optimization_barrier(probs.astype(jnp.bfloat16))
        probs_back = probs_low.astype(jnp.float32)
        attn_out = lax.optimization_barrier(jnp.einsum('gtu,ud->tgd', probs_back, value_wide).astype(jnp.bfloat16))
        delta = jnp.sum(attn_out.astype(jnp.float32) * grad_block, axis=-1)
        dprobs = jnp.einsum('tgd,ud->gtu', grad_block, value_wide)
        dscores = probs * (dprobs - delta.T[:, :, None])
        dscores_low = lax.optimization_barrier(dscores.astype(jnp.bfloat16)).astype(jnp.float32)
        query_part = (jnp.einsum('gtu,ud->tgd', dscores_low, key_wide) * score_scale).astype(jnp.bfloat16)
        key_acc = key_acc + jnp.einsum('gtu,tgd->ud', dscores_low, query_block) * score_scale
        value_acc = value_acc + jnp.einsum('gtu,tgd->ud', probs_back, grad_block)
        return (key_acc, value_acc), query_part

    empty = jnp.zeros((TOKENS, HD), jnp.float32)
    (key_acc, value_acc), query_parts = lax.scan(one_block, (empty, empty), jnp.arange(block_count, dtype=jnp.int32))
    query_out = query_parts.reshape(TOKENS, QH // KH, HD)
    return query_out, key_acc.astype(jnp.bfloat16), value_acc.astype(jnp.bfloat16)


def reference(query, key, value, out_grad, hidden_in, segment_ids):
    group_size = QH // KH
    query_heads = query.reshape(TOKENS, KH, group_size, HD).transpose(1, 0, 2, 3)
    grad_heads = out_grad.reshape(TOKENS, KH, group_size, HD).transpose(1, 0, 2, 3)
    key_heads = key.reshape(TOKENS, KH, HD).transpose(1, 0, 2)
    value_heads = value.reshape(TOKENS, KH, HD).transpose(1, 0, 2)

    def per_group(items):
        return attend_group(items[0], items[1], items[2], items[3], segment_ids)

    query_out, key_out, value_out = lax.map(per_group, (query_heads, key_heads, value_heads, grad_heads))
    query_grad = query_out.transpose(1, 0, 2, 3).reshape(TOKENS, QH * HD)
    key_grad = key_out.transpose(1, 0, 2).reshape(TOKENS, KH * HD)
    value_grad = value_out.transpose(1, 0, 2).reshape(TOKENS, KH * HD)
    weight_grad = jnp.dot(hidden_in.T, value_grad, preferred_element_type=jnp.float32)
    return query_grad, key_grad, value_grad, weight_grad
```

```python
import functools
import math

import jax
import jax.numpy as jnp
from jax import lax
from jax.experimental import pallas as pl
from jax.experimental.pallas import tpu as pltpu
from jax.sharding import PartitionSpec as P

HD = 128
TP = 4
MASKED = -1e30
MESH = pl.DeviceIdType.MESH
SEG_ROWS = 16

NT = (((1,), (1,)), ((), ()))
NN = (((1,), (0,)), ((), ()))


def dot(a, b, dims):
    return lax.dot_general(a, b, dims, preferred_element_type=jnp.float32)


def kernel(
    n, rows, heads, chunks,
    q_hbm, k_hbm, v_hbm, g_hbm, hid_hbm, seg_ref,
    dq_hbm, dk_hbm, dv_hbm, w_hbm,
    q_all, g_all, kv, bias, p_buf, dp_buf, ds_buf, pl_buf, peak, peaks, total, dtotal,
    acc, own, gout, gin, k_t, dq_v, dk_v, vg_all, vg_t, hid, w_v,
    load_sem, kvs, kvr, gs, gr, h1s, h1r, h2s, h2r, vs, vr, out_sem,
):
    half = n // 2
    per_tp = n // TP
    part = rows // TP
    width = w_v.shape[0]
    cw = heads * rows // chunks
    tile = min(256, cw)
    scale = HD ** (-0.5)
    c = lax.axis_index("ctx")
    g = lax.axis_index("tp")
    first = jnp.where(c <= half, 0, half)
    last = jnp.where(c < half, half, n - 1)
    blocks = c - first + 1
    viewers = last - c
    sibling = g + 1 - 2 * (g % 2)
    across = (g + 2) % TP
    sib_across = (sibling + 2) % TP

    k_load = pltpu.make_async_copy(k_hbm, kv.at[0, pl.ds(0, rows)], load_sem.at[0])
    v_load = pltpu.make_async_copy(v_hbm, kv.at[0, pl.ds(rows, rows)], load_sem.at[1])
    k_load.start()
    v_load.start()

    def start_head(h, _):
        cols = pl.ds(pl.multiple_of(h * HD, HD), HD)
        dst = pl.ds(pl.multiple_of(h * rows, rows), rows)
        pltpu.make_async_copy(q_hbm.at[:, cols], q_all.at[dst], load_sem.at[2]).start()
        pltpu.make_async_copy(g_hbm.at[:, cols], g_all.at[dst], load_sem.at[3]).start()
        return 0

    lax.fori_loop(0, heads, start_head, 0)
    seg = seg_ref[...].astype(jnp.float32)
    kv[0, 2 * rows :, :] = jnp.broadcast_to(seg, (SEG_ROWS, rows)).astype(jnp.bfloat16)
    k_load.wait()
    v_load.wait()

    def kv_copy(k, to):
        return pltpu.make_async_remote_copy(
            src_ref=kv.at[0], dst_ref=kv.at[k], send_sem=kvs.at[k], recv_sem=kvr.at[k],
            device_id=(to, g), device_id_type=MESH,
        )

    def kv_send(k, _):
        kv_copy(k, c + k).start()
        return 0

    lax.fori_loop(1, viewers + 1, kv_send, 0)

    def spread_remote(i, q, to):
        return pltpu.make_async_remote_copy(
            src_ref=hid_hbm.at[pl.ds(q * part, part), pl.ds(pl.multiple_of(i * width, width), width)],
            dst_ref=hid.at[c, q], send_sem=h1s.at[i * TP + q], recv_sem=h1r.at[c],
            device_id=(to, q), device_id_type=MESH,
        )

    def spread_local(i, q):
        return pltpu.make_async_copy(
            hid_hbm.at[pl.ds(q * part, part), pl.ds(pl.multiple_of(i * width, width), width)],
            hid.at[c, q], h1r.at[c],
        )

    def spread(s, _):
        i, q = s // TP, s % TP
        to = g * per_tp + i
        mine = (to == c) & (q == g)

        @pl.when(mine)
        def _():
            spread_local(i, q).start()

        @pl.when(jnp.logical_not(mine))
        def _():
            spread_remote(i, q, to).start()

        return 0

    lax.fori_loop(0, n // TP * TP, spread, 0)

    def spread_sent(s, _):
        i, q = s // TP, s % TP
        to = g * per_tp + i

        @pl.when(jnp.logical_not((to == c) & (q == g)))
        def _():
            spread_remote(i, q, to).wait_send()

        return 0

    def spread_arrived(src, _):
        mine = (src == c) & (c // per_tp == g)
        from_tp = c // per_tp

        @pl.when(mine)
        def _():
            pltpu.make_async_copy(
                hid_hbm.at[pl.ds(0, part), pl.ds(0, width)], hid.at[src, g], h1r.at[src]
            ).wait()

        @pl.when(jnp.logical_not(mine))
        def _():
            pltpu.make_async_remote_copy(
                src_ref=hid_hbm.at[pl.ds(0, part), pl.ds(0, width)], dst_ref=hid.at[src, g],
                send_sem=h1s.at[0], recv_sem=h1r.at[src],
                device_id=(src, from_tp), device_id_type=MESH,
            ).wait_recv()

        return 0

    def quarter(which, slot, to):
        return pltpu.make_async_remote_copy(
            src_ref=hid.at[:, which], dst_ref=hid.at[:, which],
            send_sem=h2s.at[slot], recv_sem=h2r.at[slot],
            device_id=(c, to), device_id_type=MESH,
        )

    pltpu.make_async_copy(q_all, q_all, load_sem.at[2]).wait()
    pltpu.make_async_copy(g_all, g_all, load_sem.at[3]).wait()
    row_iota = lax.broadcasted_iota(jnp.int32, (rows, rows), 0)
    col_iota = lax.broadcasted_iota(jnp.int32, (rows, rows), 1)

    if chunks > 1:
        acc[...] = jnp.zeros_like(acc)

        def all_arrived(k, _):
            kv_copy(k, c).wait_recv()
            return 0

        lax.fori_loop(1, blocks, all_arrived, 0)

    def clear(k, _):
        ds_buf[pl.ds(pl.multiple_of(k * rows, rows), rows), :] = jnp.zeros((rows, cw), jnp.bfloat16)
        k_t[k] = jnp.zeros((HD, rows), jnp.bfloat16)
        return 0

    lax.fori_loop(blocks, half + 1, clear, 0)

    def grad_copy(k, to):
        return pltpu.make_async_remote_copy(
            src_ref=gout.at[k], dst_ref=gin.at[k], send_sem=gs.at[k], recv_sem=gr.at[k],
            device_id=(to, g), device_id_type=MESH,
        )

    def one_chunk(chunk):
        base = 0 if chunks == 1 else pl.multiple_of(chunk * cw, cw)
        peak[...] = jnp.full_like(peak, MASKED)
        total[...] = jnp.zeros_like(total)
        dtotal[...] = jnp.zeros_like(dtotal)

        def forward(k, _):
            if chunks == 1:
                @pl.when(k > 0)
                def _():
                    kv_copy(k, c).wait_recv()

            key_seg = kv[k, 2 * rows : 2 * rows + SEG_ROWS, :][0:1, :].astype(jnp.float32)
            seg_u = jnp.broadcast_to(key_seg, (rows, rows)).T
            allowed = (seg_u == seg) & (row_iota <= col_iota + k * rows)
            one_bias = jnp.where(allowed, 0.0, MASKED)
            bias[...] = jnp.concatenate([one_bias] * (tile // rows), axis=1)
            k_t[k] = kv[k, :rows, :].T
            for at in range(0, cw, tile):
                cols = slice(at, at + tile)
                from_rows = pl.ds(base + at, tile)
                s = dot(kv[k, :rows, :], q_all[from_rows, :], NT) * (scale * math.log2(math.e)) + bias[...]
                dp = dot(kv[k, rows : 2 * rows, :], g_all[from_rows, :], NT)
                old = peak[:, cols]
                new = jnp.maximum(old, jnp.max(s, axis=0, keepdims=True))
                p = jnp.exp2(s - new)
                shrink = jnp.exp2(old - new)
                total[:, cols] = total[:, cols] * shrink + jnp.sum(p, axis=0, keepdims=True)
                dtotal[:, cols] = dtotal[:, cols] * shrink + jnp.sum(p * dp, axis=0, keepdims=True)
                peak[:, cols] = new
                peaks[k, :, cols] = new
                p_buf[k, :, cols] = p
                dp_buf[k, :, cols] = dp
            return 0

        lax.fori_loop(0, blocks, forward, 0)

        if chunks == 1:
            lax.fori_loop(0, n, spread_arrived, 0)
            quarter(g, 0, across).start()
            quarter(g, 1, sibling).start()

        total[...] = 1.0 / total[...]
        dtotal[...] = dtotal[...] * total[...]

        def backward(step, _):
            k = blocks - 1 - step
            ds_rows = pl.ds(pl.multiple_of(k * rows, rows), rows)
            for at in range(0, cw, tile):
                cols = slice(at, at + tile)
                factor = jnp.exp2(peaks[k, :, cols] - peak[:, cols]) * total[:, cols]
                p = p_buf[k, :, cols] * factor
                ds = p * (dp_buf[k, :, cols] - dtotal[:, cols])
                pl_buf[:, cols] = p.astype(jnp.bfloat16)
                ds_buf[ds_rows, cols] = ds.astype(jnp.bfloat16)
            dk = dot(ds_buf[ds_rows, :], q_all[pl.ds(base, cw), :], NN) * scale
            dv = dot(pl_buf[...], g_all[pl.ds(base, cw), :], NN)
            if chunks > 1:
                acc[k, :rows, :] += dk
                acc[k, rows:, :] += dv
            else:
                @pl.when(k > 0)
                def _():
                    gout[k, :rows, :] = dk.astype(jnp.bfloat16)
                    gout[k, rows:, :] = dv.astype(jnp.bfloat16)
                    grad_copy(k, c - k).start()

                @pl.when(k == 0)
                def _():
                    own[:rows, :] = dk
                    own[rows:, :] = dv
            return 0

        lax.fori_loop(0, blocks, backward, 0)

    def query_part(chunk):
        base = 0 if chunks == 1 else pl.multiple_of(chunk * cw, cw)
        k_flat = jnp.concatenate([k_t[k] for k in range(half + 1)], axis=1)
        for at in range(0, cw, tile):
            part_t = dot(k_flat, ds_buf[:, at : at + tile], NN) * scale
            for j in range(0, tile, rows):
                cols = pl.ds(pl.multiple_of(base + at + j, HD), HD)
                dq_v[:, cols] = part_t[:, j : j + rows].T.astype(jnp.bfloat16)

    if chunks == 1:
        one_chunk(0)
        query_part(0)
    else:
        def chunk_step(chunk, _):
            one_chunk(chunk)
            query_part(chunk)
            return 0

        lax.fori_loop(0, chunks, chunk_step, 0)

        def send_grads(step, _):
            k = blocks - 1 - step
            gout[k] = acc[k].astype(jnp.bfloat16)
            grad_copy(k, c - k).start()
            return 0

        lax.fori_loop(0, blocks - 1, send_grads, 0)
        own[...] = acc[0]
        lax.fori_loop(0, n, spread_arrived, 0)
        quarter(g, 0, across).start()
        quarter(g, 1, sibling).start()

    dq_out = pltpu.make_async_copy(dq_v, dq_hbm, out_sem.at[0])
    dq_out.start()

    def add_grads(k, _):
        grad_copy(k, c).wait_recv()
        own[...] += gin[k].astype(jnp.float32)
        return 0

    lax.fori_loop(1, viewers + 1, add_grads, 0)
    vg_all[c] = own[rows:, :].astype(jnp.bfloat16)

    def vg_copy(to, slot):
        return pltpu.make_async_remote_copy(
            src_ref=vg_all.at[slot], dst_ref=vg_all.at[slot], send_sem=vs.at[to], recv_sem=vr.at[slot],
            device_id=(to, g), device_id_type=MESH,
        )

    def vg_send(o, _):
        vg_copy((c + o) % n, c).start()
        return 0

    lax.fori_loop(1, n, vg_send, 0)
    dk_v[...] = own[:rows, :].astype(jnp.bfloat16)
    dk_out = pltpu.make_async_copy(dk_v, dk_hbm, out_sem.at[1])
    dk_out.start()
    dv_out = pltpu.make_async_copy(vg_all.at[c], dv_hbm, out_sem.at[2])
    dv_out.start()

    quarter(across, 0, across).wait_recv()
    quarter(across, 2, sibling).start()
    vg_t[c] = vg_all[c].T

    def vg_arrived(o, _):
        src = (c + o) % n
        vg_copy(src, src).wait_recv()
        vg_t[src] = vg_all[src].T
        return 0

    lax.fori_loop(1, n, vg_arrived, 0)
    quarter(sibling, 1, sibling).wait_recv()
    quarter(sib_across, 2, sibling).wait_recv()

    wt = min(256, width)
    vg_flat = jnp.concatenate([vg_t[j] for j in range(n)], axis=1)
    for at in range(0, width, wt):
        columns = hid[:, :, :, at : at + wt].reshape(n * rows, wt)
        w_t = dot(vg_flat, columns, NN)
        w_v[at : at + wt, :] = w_t.T
    w_out = pltpu.make_async_copy(w_v, w_hbm, out_sem.at[3])
    w_out.start()

    def kv_sent(k, _):
        kv_copy(k, c + k).wait_send()
        return 0

    def grads_sent(k, _):
        grad_copy(k, c - k).wait_send()
        return 0

    def vg_sent(o, _):
        vg_copy((c + o) % n, c).wait_send()
        return 0

    lax.fori_loop(1, viewers + 1, kv_sent, 0)
    lax.fori_loop(0, n // TP * TP, spread_sent, 0)
    lax.fori_loop(1, blocks, grads_sent, 0)
    lax.fori_loop(1, n, vg_sent, 0)
    quarter(g, 0, across).wait_send()
    quarter(g, 1, sibling).wait_send()
    quarter(across, 2, sibling).wait_send()
    dq_out.wait()
    dk_out.wait()
    dv_out.wait()
    w_out.wait()


def on_device(n, query, key, value, out_grad, hidden_in, segment_ids):
    rows = query.shape[0]
    heads = query.shape[1] // HD
    half = n // 2
    width = hidden_in.shape[1] * TP // n
    chunks = 1
    while (half + 1) * rows * (heads * rows // chunks) * 8 > 12 * 2**20 and heads * rows // chunks > 256:
        chunks *= 2
    cw = heads * rows // chunks
    bf, f32 = jnp.bfloat16, jnp.float32
    dma = pltpu.SemaphoreType.DMA
    vmem = pltpu.VMEM
    any_spec = pl.BlockSpec(memory_space=pl.ANY)
    acc_blocks = half + 1 if chunks > 1 else 1
    return pl.pallas_call(
        functools.partial(kernel, n, rows, heads, chunks),
        out_shape=(
            jax.ShapeDtypeStruct(query.shape, bf),
            jax.ShapeDtypeStruct(key.shape, bf),
            jax.ShapeDtypeStruct(value.shape, bf),
            jax.ShapeDtypeStruct((width, HD), f32),
        ),
        in_specs=[any_spec] * 5 + [pl.BlockSpec(memory_space=pltpu.VMEM)],
        out_specs=(any_spec,) * 4,
        scratch_shapes=[
            vmem((heads * rows, HD), bf),
            vmem((heads * rows, HD), bf),
            vmem((half + 1, 2 * rows + SEG_ROWS, HD), bf),
            vmem((rows, min(256, cw)), f32),
            vmem((half + 1, rows, cw), f32),
            vmem((half + 1, rows, cw), f32),
            vmem(((half + 1) * rows, cw), bf),
            vmem((rows, cw), bf),
            vmem((1, cw), f32),
            vmem((half + 1, 1, cw), f32),
            vmem((1, cw), f32),
            vmem((1, cw), f32),
            vmem((acc_blocks, 2 * rows, HD), f32),
            vmem((2 * rows, HD), f32),
            vmem((half + 1, 2 * rows, HD), bf),
            vmem((half + 1, 2 * rows, HD), bf),
            vmem((half + 1, HD, rows), bf),
            vmem((rows, heads * HD), bf),
            vmem((rows, HD), bf),
            vmem((n, rows, HD), bf),
            vmem((n, HD, rows), bf),
            vmem((n, TP, rows // TP, width), bf),
            vmem((width, HD), f32),
            dma((4,)),
            dma((half + 1,)),
            dma((half + 1,)),
            dma((half + 1,)),
            dma((half + 1,)),
            dma((n,)),
            dma((n,)),
            dma((3,)),
            dma((3,)),
            dma((n,)),
            dma((n,)),
            dma((4,)),
        ],
        compiler_params=pltpu.CompilerParams(
            has_side_effects=True, vmem_limit_bytes=48 * 2**20
        ),
        cost_estimate=pl.CostEstimate(flops=4 * 10**9, bytes_accessed=4 * 2**20, transcendentals=2**21),
    )(query, key, value, out_grad, hidden_in, segment_ids.reshape(1, rows))


def solution(mesh):
    return jax.shard_map(
        functools.partial(on_device, mesh.shape["ctx"]),
        mesh=mesh,
        in_specs=(
            P("ctx", "tp"),
            P("ctx", "tp"),
            P("ctx", "tp"),
            P("ctx", "tp"),
            P("ctx", "tp"),
            P("ctx"),
        ),
        out_specs=(P("ctx", "tp"), P("ctx", "tp"), P("ctx", "tp"), P("ctx", "tp")),
        check_vma=False,
    )
```

```python
import functools
import math

import jax
import jax.numpy as jnp
from jax import lax
from jax.experimental import pallas as pl
from jax.experimental.pallas import tpu as pltpu
from jax.sharding import PartitionSpec as P

HD = 128
TP = 4
MASKED = -1e30
MESH = pl.DeviceIdType.MESH
SEG_ROWS = 16

NT = (((1,), (1,)), ((), ()))
NN = (((1,), (0,)), ((), ()))


def dot(a, b, dims):
    return lax.dot_general(a, b, dims, preferred_element_type=jnp.float32)


def kernel(
    n, rows, heads, chunks,
    q_hbm, k_hbm, v_hbm, g_hbm, hid_hbm, seg_ref,
    dq_hbm, dk_hbm, dv_hbm, w_hbm,
    q_all, g_all, kv, bias, p_buf, dp_buf, ds_buf, pl_buf, peak, peaks, total, dtotal,
    acc, own, gout, gin, k_t, dq_v, dk_v, vg_all, vg_t, hid, w_v,
    load_sem, kvs, kvr, gs, gr, h1s, h1r, h2s, h2r, vs, vr, out_sem,
):
    half = n // 2
    per_tp = n // TP
    part = rows // TP
    width = w_v.shape[0]
    cw = heads * rows // chunks
    tile = min(256, cw)
    scale = HD ** (-0.5)
    c = lax.axis_index("ctx")
    g = lax.axis_index("tp")
    first = jnp.where(c <= half, 0, half)
    last = jnp.where(c < half, half, n - 1)
    blocks = c - first + 1
    viewers = last - c
    sibling = g + 1 - 2 * (g % 2)
    across = (g + 2) % TP
    sib_across = (sibling + 2) % TP

    barrier = pltpu.get_barrier_semaphore()

    def greet(d, _):
        @pl.when(d != c * TP + g)
        def _():
            pl.semaphore_signal(barrier, inc=1, device_id=(d // TP, d % TP), device_id_type=MESH)

        return 0

    lax.fori_loop(0, n * TP, greet, 0)

    k_load = pltpu.make_async_copy(k_hbm, kv.at[0, pl.ds(0, rows)], load_sem.at[0])
    v_load = pltpu.make_async_copy(v_hbm, kv.at[0, pl.ds(rows, rows)], load_sem.at[1])
    k_load.start()
    v_load.start()

    def start_head(h, _):
        cols = pl.ds(pl.multiple_of(h * HD, HD), HD)
        dst = pl.ds(pl.multiple_of(h * rows, rows), rows)
        pltpu.make_async_copy(q_hbm.at[:, cols], q_all.at[dst], load_sem.at[2]).start()
        pltpu.make_async_copy(g_hbm.at[:, cols], g_all.at[dst], load_sem.at[3]).start()
        return 0

    lax.fori_loop(0, heads, start_head, 0)
    seg = seg_ref[...].astype(jnp.float32)
    kv[0, 2 * rows :, :] = jnp.broadcast_to(seg, (SEG_ROWS, rows)).astype(jnp.bfloat16)
    k_load.wait()
    v_load.wait()
    pl.semaphore_wait(barrier, n * TP - 1)

    def kv_copy(k, to):
        return pltpu.make_async_remote_copy(
            src_ref=kv.at[0], dst_ref=kv.at[k], send_sem=kvs.at[k], recv_sem=kvr.at[k],
            device_id=(to, g), device_id_type=MESH,
        )

    def kv_send(k, _):
        kv_copy(k, c + k).start()
        return 0

    lax.fori_loop(1, viewers + 1, kv_send, 0)

    def spread_remote(i, q, to):
        return pltpu.make_async_remote_copy(
            src_ref=hid_hbm.at[pl.ds(q * part, part), pl.ds(pl.multiple_of(i * width, width), width)],
            dst_ref=hid.at[c, q], send_sem=h1s.at[i * TP + q], recv_sem=h1r.at[c],
            device_id=(to, q), device_id_type=MESH,
        )

    def spread_local(i, q):
        return pltpu.make_async_copy(
            hid_hbm.at[pl.ds(q * part, part), pl.ds(pl.multiple_of(i * width, width), width)],
            hid.at[c, q], h1r.at[c],
        )

    def spread(step, _):
        s = (step + c * (TP + 1)) % (n // TP * TP)
        i, q = s // TP, s % TP
        to = g * per_tp + i
        mine = (to == c) & (q == g)

        @pl.when(mine)
        def _():
            spread_local(i, q).start()

        @pl.when(jnp.logical_not(mine))
        def _():
            spread_remote(i, q, to).start()

        return 0

    lax.fori_loop(0, n // TP * TP, spread, 0)

    def spread_sent(s, _):
        i, q = s // TP, s % TP
        to = g * per_tp + i

        @pl.when(jnp.logical_not((to == c) & (q == g)))
        def _():
            spread_remote(i, q, to).wait_send()

        return 0

    def spread_arrived(src, _):
        mine = (src == c) & (c // per_tp == g)
        from_tp = c // per_tp

        @pl.when(mine)
        def _():
            pltpu.make_async_copy(
                hid_hbm.at[pl.ds(0, part), pl.ds(0, width)], hid.at[src, g], h1r.at[src]
            ).wait()

        @pl.when(jnp.logical_not(mine))
        def _():
            pltpu.make_async_remote_copy(
                src_ref=hid_hbm.at[pl.ds(0, part), pl.ds(0, width)], dst_ref=hid.at[src, g],
                send_sem=h1s.at[0], recv_sem=h1r.at[src],
                device_id=(src, from_tp), device_id_type=MESH,
            ).wait_recv()

        return 0

    def quarter(which, slot, to):
        return pltpu.make_async_remote_copy(
            src_ref=hid.at[:, which], dst_ref=hid.at[:, which],
            send_sem=h2s.at[slot], recv_sem=h2r.at[slot],
            device_id=(c, to), device_id_type=MESH,
        )

    pltpu.make_async_copy(q_all, q_all, load_sem.at[2]).wait()
    pltpu.make_async_copy(g_all, g_all, load_sem.at[3]).wait()
    row_iota = lax.broadcasted_iota(jnp.int32, (rows, rows), 0)
    col_iota = lax.broadcasted_iota(jnp.int32, (rows, rows), 1)

    if chunks > 1:
        acc[...] = jnp.zeros_like(acc)

        def all_arrived(k, _):
            kv_copy(k, c).wait_recv()
            return 0

        lax.fori_loop(1, blocks, all_arrived, 0)

    def clear(k, _):
        ds_buf[pl.ds(pl.multiple_of(k * rows, rows), rows), :] = jnp.zeros((rows, cw), jnp.bfloat16)
        k_t[k] = jnp.zeros((HD, rows), jnp.bfloat16)
        return 0

    lax.fori_loop(blocks, half + 1, clear, 0)

    def grad_copy(k, to):
        return pltpu.make_async_remote_copy(
            src_ref=gout.at[k], dst_ref=gin.at[k], send_sem=gs.at[k], recv_sem=gr.at[k],
            device_id=(to, g), device_id_type=MESH,
        )

    def one_chunk(chunk):
        base = 0 if chunks == 1 else pl.multiple_of(chunk * cw, cw)
        peak[...] = jnp.full_like(peak, MASKED)
        total[...] = jnp.zeros_like(total)
        dtotal[...] = jnp.zeros_like(dtotal)

        def forward(k, _):
            if chunks == 1:
                @pl.when(k > 0)
                def _():
                    kv_copy(k, c).wait_recv()

            key_seg = kv[k, 2 * rows : 2 * rows + SEG_ROWS, :][0:1, :].astype(jnp.float32)
            seg_u = jnp.broadcast_to(key_seg, (rows, rows)).T
            allowed = (seg_u == seg) & (row_iota <= col_iota + k * rows)
            one_bias = jnp.where(allowed, 0.0, MASKED)
            bias[...] = jnp.concatenate([one_bias] * (tile // rows), axis=1)
            k_t[k] = kv[k, :rows, :].T
            for at in range(0, cw, tile):
                cols = slice(at, at + tile)
                from_rows = pl.ds(base + at, tile)
                s = dot(kv[k, :rows, :], q_all[from_rows, :], NT) * (scale * math.log2(math.e)) + bias[...]
                dp = dot(kv[k, rows : 2 * rows, :], g_all[from_rows, :], NT)
                old = peak[:, cols]
                new = jnp.maximum(old, jnp.max(s, axis=0, keepdims=True))
                p = jnp.exp2(s - new)
                shrink = jnp.exp2(old - new)
                total[:, cols] = total[:, cols] * shrink + jnp.sum(p, axis=0, keepdims=True)
                dtotal[:, cols] = dtotal[:, cols] * shrink + jnp.sum(p * dp, axis=0, keepdims=True)
                peak[:, cols] = new
                peaks[k, :, cols] = new
                p_buf[k, :, cols] = p
                dp_buf[k, :, cols] = dp
            return 0

        lax.fori_loop(0, blocks, forward, 0)

        total[...] = 1.0 / total[...]
        dtotal[...] = dtotal[...] * total[...]

        def backward(step, _):
            k = blocks - 1 - step
            ds_rows = pl.ds(pl.multiple_of(k * rows, rows), rows)
            for at in range(0, cw, tile):
                cols = slice(at, at + tile)
                factor = jnp.exp2(peaks[k, :, cols] - peak[:, cols]) * total[:, cols]
                p = p_buf[k, :, cols] * factor
                ds = p * (dp_buf[k, :, cols] - dtotal[:, cols])
                pl_buf[:, cols] = p.astype(jnp.bfloat16)
                ds_buf[ds_rows, cols] = ds.astype(jnp.bfloat16)
            dk = dot(ds_buf[ds_rows, :], q_all[pl.ds(base, cw), :], NN) * scale
            dv = dot(pl_buf[...], g_all[pl.ds(base, cw), :], NN)
            if chunks > 1:
                acc[k, :rows, :] += dk
                acc[k, rows:, :] += dv
            else:
                @pl.when(k > 0)
                def _():
                    gout[k, :rows, :] = dk.astype(jnp.bfloat16)
                    gout[k, rows:, :] = dv.astype(jnp.bfloat16)
                    grad_copy(k, c - k).start()

                @pl.when(k == 0)
                def _():
                    own[:rows, :] = dk
                    own[rows:, :] = dv
            return 0

        lax.fori_loop(0, blocks, backward, 0)

    def query_part(chunk):
        base = 0 if chunks == 1 else pl.multiple_of(chunk * cw, cw)
        k_flat = jnp.concatenate([k_t[k] for k in range(half + 1)], axis=1)
        for at in range(0, cw, tile):
            part_t = dot(k_flat, ds_buf[:, at : at + tile], NN) * scale
            for j in range(0, tile, rows):
                cols = pl.ds(pl.multiple_of(base + at + j, HD), HD)
                dq_v[:, cols] = part_t[:, j : j + rows].T.astype(jnp.bfloat16)

    if chunks == 1:
        one_chunk(0)
        query_part(0)
    else:
        def chunk_step(chunk, _):
            one_chunk(chunk)
            query_part(chunk)
            return 0

        lax.fori_loop(0, chunks, chunk_step, 0)

        def send_grads(step, _):
            k = blocks - 1 - step
            gout[k] = acc[k].astype(jnp.bfloat16)
            grad_copy(k, c - k).start()
            return 0

        lax.fori_loop(0, blocks - 1, send_grads, 0)
        own[...] = acc[0]

    dq_out = pltpu.make_async_copy(dq_v, dq_hbm, out_sem.at[0])
    dq_out.start()

    lax.fori_loop(0, n, spread_arrived, 0)
    quarter(g, 0, across).start()
    quarter(g, 1, sibling).start()

    def add_grads(k, _):
        grad_copy(k, c).wait_recv()
        own[...] += gin[k].astype(jnp.float32)
        return 0

    lax.fori_loop(1, viewers + 1, add_grads, 0)
    vg_all[c] = own[rows:, :].astype(jnp.bfloat16)

    def vg_copy(to, slot):
        return pltpu.make_async_remote_copy(
            src_ref=vg_all.at[slot], dst_ref=vg_all.at[slot], send_sem=vs.at[to], recv_sem=vr.at[slot],
            device_id=(to, g), device_id_type=MESH,
        )

    def vg_send(o, _):
        vg_copy((c + o) % n, c).start()
        return 0

    lax.fori_loop(1, n, vg_send, 0)
    dk_v[...] = own[:rows, :].astype(jnp.bfloat16)
    dk_out = pltpu.make_async_copy(dk_v, dk_hbm, out_sem.at[1])
    dk_out.start()
    dv_out = pltpu.make_async_copy(vg_all.at[c], dv_hbm, out_sem.at[2])
    dv_out.start()

    quarter(across, 0, across).wait_recv()
    quarter(across, 2, sibling).start()
    vg_t[c] = vg_all[c].T

    def vg_arrived(o, _):
        src = (c + o) % n
        vg_copy(src, src).wait_recv()
        vg_t[src] = vg_all[src].T
        return 0

    lax.fori_loop(1, n, vg_arrived, 0)
    quarter(sibling, 1, sibling).wait_recv()
    quarter(sib_across, 2, sibling).wait_recv()

    wt = min(256, width)
    vg_flat = jnp.concatenate([vg_t[j] for j in range(n)], axis=1)
    for at in range(0, width, wt):
        columns = hid[:, :, :, at : at + wt].reshape(n * rows, wt)
        w_t = dot(vg_flat, columns, NN)
        w_v[at : at + wt, :] = w_t.T
    w_out = pltpu.make_async_copy(w_v, w_hbm, out_sem.at[3])
    w_out.start()

    def kv_sent(k, _):
        kv_copy(k, c + k).wait_send()
        return 0

    def grads_sent(k, _):
        grad_copy(k, c - k).wait_send()
        return 0

    def vg_sent(o, _):
        vg_copy((c + o) % n, c).wait_send()
        return 0

    lax.fori_loop(1, viewers + 1, kv_sent, 0)
    lax.fori_loop(0, n // TP * TP, spread_sent, 0)
    lax.fori_loop(1, blocks, grads_sent, 0)
    lax.fori_loop(1, n, vg_sent, 0)
    quarter(g, 0, across).wait_send()
    quarter(g, 1, sibling).wait_send()
    quarter(across, 2, sibling).wait_send()
    dq_out.wait()
    dk_out.wait()
    dv_out.wait()
    w_out.wait()


def on_device(n, query, key, value, out_grad, hidden_in, segment_ids):
    rows = query.shape[0]
    heads = query.shape[1] // HD
    half = n // 2
    width = hidden_in.shape[1] * TP // n
    chunks = 1
    while (half + 1) * rows * (heads * rows // chunks) * 8 > 12 * 2**20 and heads * rows // chunks > 256:
        chunks *= 2
    cw = heads * rows // chunks
    bf, f32 = jnp.bfloat16, jnp.float32
    dma = pltpu.SemaphoreType.DMA
    vmem = pltpu.VMEM
    any_spec = pl.BlockSpec(memory_space=pl.ANY)
    acc_blocks = half + 1 if chunks > 1 else 1
    results = pl.pallas_call(
        functools.partial(kernel, n, rows, heads, chunks),
        out_shape=(
            jax.ShapeDtypeStruct(query.shape, bf),
            jax.ShapeDtypeStruct(key.shape, bf),
            jax.ShapeDtypeStruct(value.shape, bf),
            jax.ShapeDtypeStruct((width, HD), f32),
        ),
        in_specs=[any_spec] * 5 + [pl.BlockSpec(memory_space=pltpu.VMEM)],
        out_specs=(any_spec,) * 4,
        scratch_shapes=[
            vmem((heads * rows, HD), bf),
            vmem((heads * rows, HD), bf),
            vmem((half + 1, 2 * rows + SEG_ROWS, HD), bf),
            vmem((rows, min(256, cw)), f32),
            vmem((half + 1, rows, cw), f32),
            vmem((half + 1, rows, cw), f32),
            vmem(((half + 1) * rows, cw), bf),
            vmem((rows, cw), bf),
            vmem((1, cw), f32),
            vmem((half + 1, 1, cw), f32),
            vmem((1, cw), f32),
            vmem((1, cw), f32),
            vmem((acc_blocks, 2 * rows, HD), f32),
            vmem((2 * rows, HD), f32),
            vmem((half + 1, 2 * rows, HD), bf),
            vmem((half + 1, 2 * rows, HD), bf),
            vmem((half + 1, HD, rows), bf),
            vmem((rows, heads * HD), bf),
            vmem((rows, HD), bf),
            vmem((n, rows, HD), bf),
            vmem((n, HD, rows), bf),
            vmem((n, TP, rows // TP, width), bf),
            vmem((width, HD), f32),
            dma((4,)),
            dma((half + 1,)),
            dma((half + 1,)),
            dma((half + 1,)),
            dma((half + 1,)),
            dma((n,)),
            dma((n,)),
            dma((3,)),
            dma((3,)),
            dma((n,)),
            dma((n,)),
            dma((4,)),
        ],
        compiler_params=pltpu.CompilerParams(
            has_side_effects=True, vmem_limit_bytes=62 * 2**20, collective_id=0
        ),
        cost_estimate=pl.CostEstimate(flops=4 * 10**9, bytes_accessed=4 * 2**20, transcendentals=2**21),
    )(query, key, value, out_grad, hidden_in, segment_ids.reshape(1, rows))
    return results


def solution(mesh):
    return jax.shard_map(
        functools.partial(on_device, mesh.shape["ctx"]),
        mesh=mesh,
        in_specs=(
            P("ctx", "tp"),
            P("ctx", "tp"),
            P("ctx", "tp"),
            P("ctx", "tp"),
            P("ctx", "tp"),
            P("ctx"),
        ),
        out_specs=(P("ctx", "tp"), P("ctx", "tp"), P("ctx", "tp"), P("ctx", "tp")),
        check_vma=False,
    )
```

```python
import functools
import math

import jax
import jax.numpy as jnp
from jax import lax
from jax.experimental import pallas as pl
from jax.experimental.pallas import tpu as pltpu
from jax.sharding import PartitionSpec as P

HD = 128
TP = 4
MASKED = -1e30
MESH = pl.DeviceIdType.MESH
SEG_ROWS = 16

NT = (((1,), (1,)), ((), ()))
NN = (((1,), (0,)), ((), ()))


def dot(a, b, dims):
    return lax.dot_general(a, b, dims, preferred_element_type=jnp.float32)


def kernel(
    n, rows, heads, chunks,
    q_hbm, k_hbm, v_hbm, g_hbm, hid_hbm, seg_ref,
    dq_hbm, dk_hbm, dv_hbm, w_hbm,
    q_all, g_all, kv, bias, p_buf, dp_buf, ds_buf, pl_buf, peak, peaks, total, dtotal,
    acc, own, gout, gin, k_t, dq_v, dk_v, vg_all, vg_t, hid, w_v,
    load_sem, kvs, kvr, gs, gr, h1s, h1r, h2s, h2r, vs, vr, out_sem,
):
    half = n // 2
    per_tp = n // TP
    part = rows // TP
    width = w_v.shape[0]
    cw = heads * rows // chunks
    tile = min(256, cw)
    scale = HD ** (-0.5)
    c = lax.axis_index("ctx")
    g = lax.axis_index("tp")
    first = jnp.where(c <= half, 0, half)
    last = jnp.where(c < half, half, n - 1)
    blocks = c - first + 1
    viewers = last - c
    sibling = g + 1 - 2 * (g % 2)
    across = (g + 2) % TP
    sib_across = (sibling + 2) % TP

    barrier = pltpu.get_barrier_semaphore()

    def greet(d, _):
        @pl.when(d != c * TP + g)
        def _():
            pl.semaphore_signal(barrier, inc=1, device_id=(d // TP, d % TP), device_id_type=MESH)

        return 0

    lax.fori_loop(0, n * TP, greet, 0)

    k_load = pltpu.make_async_copy(k_hbm, kv.at[0, pl.ds(0, rows)], load_sem.at[0])
    v_load = pltpu.make_async_copy(v_hbm, kv.at[0, pl.ds(rows, rows)], load_sem.at[1])
    k_load.start()
    v_load.start()

    def start_head(h, _):
        cols = pl.ds(pl.multiple_of(h * HD, HD), HD)
        dst = pl.ds(pl.multiple_of(h * rows, rows), rows)
        pltpu.make_async_copy(q_hbm.at[:, cols], q_all.at[dst], load_sem.at[2]).start()
        pltpu.make_async_copy(g_hbm.at[:, cols], g_all.at[dst], load_sem.at[3]).start()
        return 0

    lax.fori_loop(0, heads, start_head, 0)
    seg = seg_ref[...].astype(jnp.float32)
    kv[0, 2 * rows :, :] = jnp.broadcast_to(seg, (SEG_ROWS, rows)).astype(jnp.bfloat16)
    k_load.wait()
    v_load.wait()
    pl.semaphore_wait(barrier, n * TP - 1)

    def kv_copy(k, to):
        return pltpu.make_async_remote_copy(
            src_ref=kv.at[0], dst_ref=kv.at[k], send_sem=kvs.at[k], recv_sem=kvr.at[k],
            device_id=(to, g), device_id_type=MESH,
        )

    def kv_send(k, _):
        kv_copy(k, c + k).start()
        return 0

    lax.fori_loop(1, viewers + 1, kv_send, 0)

    def spread_remote(i, q, to):
        return pltpu.make_async_remote_copy(
            src_ref=hid_hbm.at[pl.ds(q * part, part), pl.ds(pl.multiple_of(i * width, width), width)],
            dst_ref=hid.at[c, q], send_sem=h1s.at[i * TP + q], recv_sem=h1r.at[c],
            device_id=(to, q), device_id_type=MESH,
        )

    def spread_local(i, q):
        return pltpu.make_async_copy(
            hid_hbm.at[pl.ds(q * part, part), pl.ds(pl.multiple_of(i * width, width), width)],
            hid.at[c, q], h1r.at[c],
        )

    def spread(step, _):
        s = (step + c * (TP + 1)) % (n // TP * TP)
        i, q = s // TP, s % TP
        to = g * per_tp + i
        mine = (to == c) & (q == g)

        @pl.when(mine)
        def _():
            spread_local(i, q).start()

        @pl.when(jnp.logical_not(mine))
        def _():
            spread_remote(i, q, to).start()

        return 0

    lax.fori_loop(0, n // TP * TP, spread, 0)

    def spread_sent(s, _):
        i, q = s // TP, s % TP
        to = g * per_tp + i

        @pl.when(jnp.logical_not((to == c) & (q == g)))
        def _():
            spread_remote(i, q, to).wait_send()

        return 0

    def spread_arrived(src, _):
        mine = (src == c) & (c // per_tp == g)
        from_tp = c // per_tp

        @pl.when(mine)
        def _():
            pltpu.make_async_copy(
                hid_hbm.at[pl.ds(0, part), pl.ds(0, width)], hid.at[src, g], h1r.at[src]
            ).wait()

        @pl.when(jnp.logical_not(mine))
        def _():
            pltpu.make_async_remote_copy(
                src_ref=hid_hbm.at[pl.ds(0, part), pl.ds(0, width)], dst_ref=hid.at[src, g],
                send_sem=h1s.at[0], recv_sem=h1r.at[src],
                device_id=(src, from_tp), device_id_type=MESH,
            ).wait_recv()

        return 0

    near = c // half * half

    def quarter(which, slot, to, turn):
        sources = pl.ds(near if turn == 0 else half - near, half)
        return pltpu.make_async_remote_copy(
            src_ref=hid.at[sources, which], dst_ref=hid.at[sources, which],
            send_sem=h2s.at[3 * turn + slot], recv_sem=h2r.at[3 * turn + slot],
            device_id=(c, to), device_id_type=MESH,
        )

    pltpu.make_async_copy(q_all, q_all, load_sem.at[2]).wait()
    pltpu.make_async_copy(g_all, g_all, load_sem.at[3]).wait()
    row_iota = lax.broadcasted_iota(jnp.int32, (rows, rows), 0)
    col_iota = lax.broadcasted_iota(jnp.int32, (rows, rows), 1)

    if chunks > 1:
        acc[...] = jnp.zeros_like(acc)

        def all_arrived(k, _):
            kv_copy(k, c).wait_recv()
            return 0

        lax.fori_loop(1, blocks, all_arrived, 0)

    def clear(k, _):
        ds_buf[pl.ds(pl.multiple_of(k * rows, rows), rows), :] = jnp.zeros((rows, cw), jnp.bfloat16)
        k_t[k] = jnp.zeros((HD, rows), jnp.bfloat16)
        return 0

    lax.fori_loop(blocks, half + 1, clear, 0)

    def grad_copy(k, to):
        return pltpu.make_async_remote_copy(
            src_ref=gout.at[k], dst_ref=gin.at[k], send_sem=gs.at[k], recv_sem=gr.at[k],
            device_id=(to, g), device_id_type=MESH,
        )

    def one_chunk(chunk):
        base = 0 if chunks == 1 else pl.multiple_of(chunk * cw, cw)
        peak[...] = jnp.full_like(peak, MASKED)
        total[...] = jnp.zeros_like(total)
        dtotal[...] = jnp.zeros_like(dtotal)

        def forward(k, _):
            if chunks == 1:
                @pl.when(k > 0)
                def _():
                    kv_copy(k, c).wait_recv()

            key_seg = kv[k, 2 * rows : 2 * rows + SEG_ROWS, :][0:1, :].astype(jnp.float32)
            seg_u = jnp.broadcast_to(key_seg, (rows, rows)).T
            allowed = (seg_u == seg) & (row_iota <= col_iota + k * rows)
            one_bias = jnp.where(allowed, 0.0, MASKED)
            bias[...] = jnp.concatenate([one_bias] * (tile // rows), axis=1)
            k_t[k] = kv[k, :rows, :].T
            for at in range(0, cw, tile):
                cols = slice(at, at + tile)
                from_rows = pl.ds(base + at, tile)
                s = dot(kv[k, :rows, :], q_all[from_rows, :], NT) * (scale * math.log2(math.e)) + bias[...]
                dp = dot(kv[k, rows : 2 * rows, :], g_all[from_rows, :], NT)
                old = peak[:, cols]
                new = jnp.maximum(old, jnp.max(s, axis=0, keepdims=True))
                p = jnp.exp2(s - new)
                shrink = jnp.exp2(old - new)
                total[:, cols] = total[:, cols] * shrink + jnp.sum(p, axis=0, keepdims=True)
                dtotal[:, cols] = dtotal[:, cols] * shrink + jnp.sum(p * dp, axis=0, keepdims=True)
                peak[:, cols] = new
                peaks[k, :, cols] = new
                p_buf[k, :, cols] = p
                dp_buf[k, :, cols] = dp
            return 0

        lax.fori_loop(0, blocks, forward, 0)

        total[...] = 1.0 / total[...]
        dtotal[...] = dtotal[...] * total[...]

        def backward(step, _):
            k = blocks - 1 - step
            ds_rows = pl.ds(pl.multiple_of(k * rows, rows), rows)
            for at in range(0, cw, tile):
                cols = slice(at, at + tile)
                factor = jnp.exp2(peaks[k, :, cols] - peak[:, cols]) * total[:, cols]
                p = p_buf[k, :, cols] * factor
                ds = p * (dp_buf[k, :, cols] - dtotal[:, cols])
                pl_buf[:, cols] = p.astype(jnp.bfloat16)
                ds_buf[ds_rows, cols] = ds.astype(jnp.bfloat16)
            dk = dot(ds_buf[ds_rows, :], q_all[pl.ds(base, cw), :], NN) * scale
            dv = dot(pl_buf[...], g_all[pl.ds(base, cw), :], NN)
            if chunks > 1:
                acc[k, :rows, :] += dk
                acc[k, rows:, :] += dv
            else:
                @pl.when(k > 0)
                def _():
                    gout[k, :rows, :] = dk.astype(jnp.bfloat16)
                    gout[k, rows:, :] = dv.astype(jnp.bfloat16)
                    grad_copy(k, c - k).start()

                @pl.when(k == 0)
                def _():
                    own[:rows, :] = dk
                    own[rows:, :] = dv
            return 0

        lax.fori_loop(0, blocks, backward, 0)

    def query_part(chunk):
        base = 0 if chunks == 1 else pl.multiple_of(chunk * cw, cw)
        k_flat = jnp.concatenate([k_t[k] for k in range(half + 1)], axis=1)
        for at in range(0, cw, tile):
            part_t = dot(k_flat, ds_buf[:, at : at + tile], NN) * scale
            for j in range(0, tile, rows):
                cols = pl.ds(pl.multiple_of(base + at + j, HD), HD)
                dq_v[:, cols] = part_t[:, j : j + rows].T.astype(jnp.bfloat16)

    if chunks == 1:
        one_chunk(0)
        lax.fori_loop(near, near + half, spread_arrived, 0)
        quarter(g, 0, across, 0).start()
        quarter(g, 1, sibling, 0).start()
        query_part(0)
    else:
        def chunk_step(chunk, _):
            one_chunk(chunk)
            query_part(chunk)
            return 0

        lax.fori_loop(0, chunks, chunk_step, 0)

        def send_grads(step, _):
            k = blocks - 1 - step
            gout[k] = acc[k].astype(jnp.bfloat16)
            grad_copy(k, c - k).start()
            return 0

        lax.fori_loop(0, blocks - 1, send_grads, 0)
        own[...] = acc[0]
        lax.fori_loop(near, near + half, spread_arrived, 0)
        quarter(g, 0, across, 0).start()
        quarter(g, 1, sibling, 0).start()

    dq_out = pltpu.make_async_copy(dq_v, dq_hbm, out_sem.at[0])
    dq_out.start()

    lax.fori_loop(half - near, n - near, spread_arrived, 0)
    quarter(g, 0, across, 1).start()
    quarter(g, 1, sibling, 1).start()

    def add_grads(k, _):
        grad_copy(k, c).wait_recv()
        own[...] += gin[k].astype(jnp.float32)
        return 0

    lax.fori_loop(1, viewers + 1, add_grads, 0)
    vg_all[c] = own[rows:, :].astype(jnp.bfloat16)

    def vg_copy(to, slot):
        return pltpu.make_async_remote_copy(
            src_ref=vg_all.at[slot], dst_ref=vg_all.at[slot], send_sem=vs.at[to], recv_sem=vr.at[slot],
            device_id=(to, g), device_id_type=MESH,
        )

    def vg_send(o, _):
        vg_copy((c + o) % n, c).start()
        return 0

    lax.fori_loop(1, n, vg_send, 0)
    dk_v[...] = own[:rows, :].astype(jnp.bfloat16)
    dk_out = pltpu.make_async_copy(dk_v, dk_hbm, out_sem.at[1])
    dk_out.start()
    dv_out = pltpu.make_async_copy(vg_all.at[c], dv_hbm, out_sem.at[2])
    dv_out.start()

    quarter(across, 0, across, 0).wait_recv()
    quarter(across, 2, sibling, 0).start()
    quarter(across, 0, across, 1).wait_recv()
    quarter(across, 2, sibling, 1).start()
    vg_t[c] = vg_all[c].T

    def vg_arrived(o, _):
        src = (c + o) % n
        vg_copy(src, src).wait_recv()
        vg_t[src] = vg_all[src].T
        return 0

    lax.fori_loop(1, n, vg_arrived, 0)
    quarter(sibling, 1, sibling, 0).wait_recv()
    quarter(sibling, 1, sibling, 1).wait_recv()
    quarter(sib_across, 2, sibling, 0).wait_recv()
    quarter(sib_across, 2, sibling, 1).wait_recv()

    wt = min(256, width)
    vg_flat = jnp.concatenate([vg_t[j] for j in range(n)], axis=1)
    for at in range(0, width, wt):
        columns = hid[:, :, :, at : at + wt].reshape(n * rows, wt)
        w_t = dot(vg_flat, columns, NN)
        w_v[at : at + wt, :] = w_t.T
    w_out = pltpu.make_async_copy(w_v, w_hbm, out_sem.at[3])
    w_out.start()

    def kv_sent(k, _):
        kv_copy(k, c + k).wait_send()
        return 0

    def grads_sent(k, _):
        grad_copy(k, c - k).wait_send()
        return 0

    def vg_sent(o, _):
        vg_copy((c + o) % n, c).wait_send()
        return 0

    lax.fori_loop(1, viewers + 1, kv_sent, 0)
    lax.fori_loop(0, n // TP * TP, spread_sent, 0)
    lax.fori_loop(1, blocks, grads_sent, 0)
    lax.fori_loop(1, n, vg_sent, 0)
    quarter(g, 0, across, 0).wait_send()
    quarter(g, 0, across, 1).wait_send()
    quarter(g, 1, sibling, 0).wait_send()
    quarter(g, 1, sibling, 1).wait_send()
    quarter(across, 2, sibling, 0).wait_send()
    quarter(across, 2, sibling, 1).wait_send()
    dq_out.wait()
    dk_out.wait()
    dv_out.wait()
    w_out.wait()


def on_device(n, query, key, value, out_grad, hidden_in, segment_ids):
    rows = query.shape[0]
    heads = query.shape[1] // HD
    half = n // 2
    width = hidden_in.shape[1] * TP // n
    chunks = 1
    while (half + 1) * rows * (heads * rows // chunks) * 8 > 12 * 2**20 and heads * rows // chunks > 256:
        chunks *= 2
    cw = heads * rows // chunks
    bf, f32 = jnp.bfloat16, jnp.float32
    dma = pltpu.SemaphoreType.DMA
    vmem = pltpu.VMEM
    any_spec = pl.BlockSpec(memory_space=pl.ANY)
    acc_blocks = half + 1 if chunks > 1 else 1
    results = pl.pallas_call(
        functools.partial(kernel, n, rows, heads, chunks),
        out_shape=(
            jax.ShapeDtypeStruct(query.shape, bf),
            jax.ShapeDtypeStruct(key.shape, bf),
            jax.ShapeDtypeStruct(value.shape, bf),
            jax.ShapeDtypeStruct((width, HD), f32),
        ),
        in_specs=[any_spec] * 5 + [pl.BlockSpec(memory_space=pltpu.VMEM)],
        out_specs=(any_spec,) * 4,
        scratch_shapes=[
            vmem((heads * rows, HD), bf),
            vmem((heads * rows, HD), bf),
            vmem((half + 1, 2 * rows + SEG_ROWS, HD), bf),
            vmem((rows, min(256, cw)), f32),
            vmem((half + 1, rows, cw), f32),
            vmem((half + 1, rows, cw), f32),
            vmem(((half + 1) * rows, cw), bf),
            vmem((rows, cw), bf),
            vmem((1, cw), f32),
            vmem((half + 1, 1, cw), f32),
            vmem((1, cw), f32),
            vmem((1, cw), f32),
            vmem((acc_blocks, 2 * rows, HD), f32),
            vmem((2 * rows, HD), f32),
            vmem((half + 1, 2 * rows, HD), bf),
            vmem((half + 1, 2 * rows, HD), bf),
            vmem((half + 1, HD, rows), bf),
            vmem((rows, heads * HD), bf),
            vmem((rows, HD), bf),
            vmem((n, rows, HD), bf),
            vmem((n, HD, rows), bf),
            vmem((n, TP, rows // TP, width), bf),
            vmem((width, HD), f32),
            dma((4,)),
            dma((half + 1,)),
            dma((half + 1,)),
            dma((half + 1,)),
            dma((half + 1,)),
            dma((n,)),
            dma((n,)),
            dma((6,)),
            dma((6,)),
            dma((n,)),
            dma((n,)),
            dma((4,)),
        ],
        compiler_params=pltpu.CompilerParams(
            has_side_effects=True, vmem_limit_bytes=62 * 2**20, collective_id=0
        ),
        cost_estimate=pl.CostEstimate(flops=4 * 10**9, bytes_accessed=4 * 2**20, transcendentals=2**21),
    )(query, key, value, out_grad, hidden_in, segment_ids.reshape(1, rows))
    return results


def solution(mesh):
    return jax.shard_map(
        functools.partial(on_device, mesh.shape["ctx"]),
        mesh=mesh,
        in_specs=(
            P("ctx", "tp"),
            P("ctx", "tp"),
            P("ctx", "tp"),
            P("ctx", "tp"),
            P("ctx", "tp"),
            P("ctx"),
        ),
        out_specs=(P("ctx", "tp"), P("ctx", "tp"), P("ctx", "tp"), P("ctx", "tp")),
        check_vma=False,
    )
```
